32 devices in a mesh: seq: 16 (over z, y, core), ch: 2 (over x).
Axes of the slice: x: 2, y: 2, z: 4, core: 2. Of those that a mesh axis runs over, the one named last changes fastest.
Arguments:
- tokens: int32 [4096], P('seq'), may hold values from 0 to 3
- feature_table: bfloat16 [512, 3, 4096], P(None, None, 'ch'), may hold values from -6 to 6
- short_filter: float32 [3, 7, 4096], P(None, None, 'ch'), may hold values from -2 to 2
- med_filter: bfloat16 [128, 256], P(None, 'ch'), may hold values from -0.5 to 0.5
- med_bias: float32 [4096], P('ch'), may hold values from 0.5 to 1.5
- out_weight: bfloat16 [4096, 4096], P('seq', 'ch'), may hold values from -0.09375 to 0.09375
Outputs:
- scored: bfloat16 [4096, 4096], P('seq', 'ch')
The draws below stay inside these ranges and needn't reach their ends.
All inputs are finite; a program needn't handle non-finite values.
Results may differ from the reference program's by a relative error of at most 0.01.
Values may be sent and summed in bfloat16 or wider, within the bound.
A program may use at most 128 MiB of HBM per device.

```python
import jax
import jax.numpy as jnp
import numpy as np
from jax import lax

D = 4096
VOCAB = 512
SHORT = 7
MTAPS = 128
GROUP = 16
NGROUPS = 256
SEQ = 4096


def touch_ends(drawn, rng, low, high):
    longest = drawn.shape.index(max(drawn.shape))
    spots = []
    for shift in (0, 1):
        where = [jax.random.randint(jax.random.fold_in(rng, axis), (), 0, length) for axis, length in enumerate(drawn.shape)]
        where[longest] = (where[longest] + shift) % drawn.shape[longest]
        spots.append(tuple(where))
    return drawn.at[spots[0]].set(low).at[spots[1]].set(high)


def levels(rng, extent, shards, smallest, top_value):
    def one(position, parts):
        heights = jax.random.uniform(jax.random.fold_in(jax.random.fold_in(rng, 6), position), (parts,), jnp.float32, smallest / len(shards), top_value / len(shards))
        return jnp.repeat(jnp.exp(heights), extent[position] // parts).reshape((-1,) + (1,) * (len(extent) - position - 1))

    gain = one(*shards[0])
    for cut in shards[1:]:
        gain = gain * one(*cut)
    return gain


def noise(stream_key, dims, deviation, limit, shards=(), kind=jnp.bfloat16):
    values = deviation * jax.random.normal(stream_key, dims, jnp.float32)
    if shards:
        values = values * levels(stream_key, dims, shards, -0.22, 0.18)
    return jnp.clip(values, -limit, limit).astype(kind)


def setup_inputs(seed: int = 0) -> dict:
    arg_keys = jax.random.split(jax.random.key(seed), 7)
    return {
        "tokens": touch_ends(jax.random.randint(arg_keys[0], (SEQ,), 0, 4), jax.random.fold_in(arg_keys[0], 1), 0, 3).astype(jnp.int32),
        "feature_table": noise(arg_keys[1], (VOCAB, 3, D), 1.0, 6.0, ((2, 2),)),
        "short_filter": noise(arg_keys[2], (3, SHORT, D), SHORT ** -0.5, 2.0, ((2, 2),), jnp.float32),
        "med_filter": noise(arg_keys[3], (MTAPS, NGROUPS), MTAPS ** -0.5, 0.5, ((1, 2),)),
        "med_bias": jnp.clip(0.5 + 1.0 * jax.random.uniform(arg_keys[4], (D,), jnp.float32) ** levels(arg_keys[4], (D,), ((0, 2),), -0.2, 0.2), 0.5, 1.5),
        "out_weight": noise(arg_keys[5], (D, D), D ** -0.5, 0.09375, ((0, 16), (1, 2))),
    }


base_codes = np.array([65, 67, 71, 84], dtype=np.int32)


def toeplitz(filters):
    tap_count = filters.shape[0]
    row_index = jnp.arange(tap_count, dtype=jnp.int32)[:, None]
    col_index = jnp.arange(2 * tap_count - 1, dtype=jnp.int32)[None, :]
    tap_index = row_index - col_index + tap_count - 1
    inside = (tap_index >= 0) & (tap_index < tap_count)
    picked = jnp.take(filters.astype(jnp.float32), jnp.clip(tap_index, 0, tap_count - 1), axis=0)
    toeplitz_table = jnp.where(inside[:, :, None], picked, jnp.float32(0.0))
    return jnp.transpose(toeplitz_table, (2, 0, 1))


def medium_conv(gated_mix, filters):
    tap_count = filters.shape[0]
    groups = filters.shape[1]
    channels = gated_mix.shape[1]
    group_width = channels // groups
    kernel = toeplitz(filters)
    padded = jnp.concatenate([jnp.zeros((tap_count - 1, channels), jnp.float32), gated_mix.astype(jnp.float32)], axis=0)

    def one_block(block_index):
        window = lax.dynamic_slice_in_dim(padded, block_index * tap_count, 2 * tap_count - 1, 0)
        window = window.reshape(2 * tap_count - 1, groups, group_width)
        product = jnp.einsum("grw,wgc->rgc", kernel, window, precision=lax.Precision.HIGHEST)
        return product.reshape(tap_count, channels)

    blocks = lax.map(one_block, jnp.arange(gated_mix.shape[0] // tap_count, dtype=jnp.int32))
    return blocks.reshape(gated_mix.shape[0], channels)


def strand_hidden(strand_bases, feature_table, short_filter, med_filter, med_bias):
    block_width = min(D, 512)
    group_block = block_width // GROUP

    def one_slab(slab_index):
        offset = slab_index * block_width
        table_part = lax.dynamic_slice_in_dim(feature_table, offset, block_width, 2)
        short_part = lax.dynamic_slice_in_dim(short_filter, offset, block_width, 2)
        medium_part = lax.dynamic_slice_in_dim(med_filter, slab_index * group_block, group_block, 1)
        bias_part = lax.dynamic_slice_in_dim(med_bias, offset, block_width, 0)
        corner = table_part[base_codes]
        features = jnp.take(corner, strand_bases, axis=0).astype(jnp.float32)
        padded = jnp.pad(features, ((SHORT - 1, 0), (0, 0), (0, 0)))
        short_out = jnp.zeros((SEQ, 3, block_width), jnp.float32)
        for shift_index in range(SHORT):
            begin = SHORT - 1 - shift_index
            short_out = short_out + short_part[:, shift_index, :] * padded[begin:begin + SEQ]
        gated_mix = (short_out[:, 0] * short_out[:, 2]).astype(jnp.bfloat16)
        medium = medium_conv(gated_mix, medium_part) + bias_part * gated_mix.astype(jnp.float32)
        return (short_out[:, 1] * medium).astype(jnp.bfloat16)

    slabs = lax.map(one_slab, jnp.arange(D // block_width, dtype=jnp.int32))
    return jnp.transpose(slabs, (1, 0, 2)).reshape(SEQ, D)


def reference(tokens, feature_table, short_filter, med_filter, med_bias, out_weight):
    forward = strand_hidden(tokens, feature_table, short_filter, med_filter, med_bias)
    reverse = strand_hidden(3 - jnp.flip(tokens, 0), feature_table, short_filter, med_filter, med_bias)
    averaged = (0.5 * (forward.astype(jnp.float32) + jnp.flip(reverse, 0).astype(jnp.float32))).astype(jnp.bfloat16)
    return jnp.dot(averaged, out_weight, preferred_element_type=jnp.float32).astype(jnp.bfloat16)
```

```python
import functools

import jax
import jax.numpy as jnp
from jax import lax
from jax.experimental import pallas as pl
from jax.experimental.pallas import tpu as pltpu
from jax.sharding import PartitionSpec as P

BASE_CODES = (65, 67, 71, 84)
LANES = 128


def hidden_kernel(taps, group_width, hot_f, hot_r, coef, base_f, base_r, bias, out):
    length = out.shape[0]
    blocks = length // taps
    groups = LANES // group_width
    lane_group = lax.broadcasted_iota(jnp.int32, (taps, LANES), 1) // group_width

    def dot(a, b):
        return jnp.dot(a, b, preferred_element_type=jnp.float32)

    def strand(hot, base, first):
        rows = hot[...]
        gate = (dot(rows, coef[0]) * dot(rows, coef[2])).astype(jnp.bfloat16)
        middle = dot(rows[first : first + length], coef[1])
        window = jnp.concatenate(
            [gate[n * taps : (n + 2) * taps] for n in range(blocks)], axis=1
        )
        mixed = [jnp.zeros((taps, LANES), jnp.float32) for _ in range(blocks)]
        for g in range(groups):
            row = jnp.broadcast_to(base[0, g : g + 1, :], (taps, 2 * taps))
            toeplitz = pltpu.roll(row, 0, 1, stride=1, stride_axis=0).astype(jnp.bfloat16)
            product = dot(toeplitz, window)
            for n in range(blocks):
                mixed[n] = jnp.where(
                    lane_group == g, product[:, n * LANES : (n + 1) * LANES], mixed[n]
                )
        own = gate[first : first + length].astype(jnp.float32)
        total = jnp.concatenate(mixed, axis=0) + bias[0] * own
        return (middle * total).astype(jnp.bfloat16).astype(jnp.float32)

    forward = strand(hot_f, base_f, taps)
    reverse = strand(hot_r, base_r, 0)
    out[...] = (0.5 * (forward + reverse)).astype(jnp.bfloat16)


def one_hot(codes, offset, count, step, short_taps):
    picked = jnp.stack(
        [codes[offset + step * k : offset + step * k + count] for k in range(short_taps)], axis=1
    )
    hot = (picked[:, :, None] == jnp.arange(4, dtype=jnp.int32)).astype(jnp.bfloat16)
    hot = hot.reshape(count, 4 * short_taps)
    return jnp.pad(jnp.concatenate([hot, hot], 1), ((0, 0), (0, LANES - 8 * short_taps)))


def coefficients(feature_table, short_filter):
    corner = jnp.stack([feature_table[code] for code in BASE_CODES])
    product = short_filter[:, :, None, :] * jnp.transpose(corner, (1, 0, 2)).astype(jnp.float32)[:, None]
    product = product.reshape(3, -1, product.shape[-1])
    high = lax.reduce_precision(product, 8, 7)
    low = (product - high).astype(jnp.bfloat16)
    both = jnp.concatenate([high.astype(jnp.bfloat16), low], axis=1)
    return jnp.pad(both, ((0, 0), (0, LANES - both.shape[1]), (0, 0)))


def hidden(tokens, base_rows, coef, bias, taps, group_width, short_taps, size):
    length = tokens.shape[0]
    index = lax.axis_index("seq")
    before = lax.ppermute(tokens, "seq", [(i, i + 1) for i in range(size - 1)])
    after = lax.ppermute(tokens, "seq", [(i + 1, i) for i in range(size - 1)])
    before = jnp.where(index == 0, -1, before)
    after = jnp.where(index == size - 1, -1, after)
    codes = jnp.concatenate([before, tokens, after])
    flipped = jnp.where(codes < 0, -1, 3 - codes)
    window = length + taps
    hot_f = one_hot(codes, length - taps, window, -1, short_taps)
    hot_r = one_hot(flipped, length, window, 1, short_taps)
    width = coef.shape[2]
    groups = LANES // group_width
    steps = width // LANES
    whole = pl.BlockSpec((window, LANES), lambda i: (0, 0))
    rows = pl.BlockSpec((1, groups, 2 * taps), lambda i: (i, 0, 0))
    return pl.pallas_call(
        functools.partial(hidden_kernel, taps, group_width),
        out_shape=jax.ShapeDtypeStruct((length, width), jnp.bfloat16),
        grid=(steps,),
        in_specs=[
            whole,
            whole,
            pl.BlockSpec((3, LANES, LANES), lambda i: (0, 0, i)),
            rows,
            rows,
            pl.BlockSpec((1, 1, LANES), lambda i: (i, 0, 0)),
        ],
        out_specs=pl.BlockSpec((length, LANES), lambda i: (0, i)),
        compiler_params=pltpu.CompilerParams(vmem_limit_bytes=32 * 1024 * 1024),
        cost_estimate=pl.CostEstimate(
            flops=2 * 2 * length * width * 2 * taps * groups, bytes_accessed=8 * 1024 * 1024, transcendentals=0
        ),
    )(hot_f, hot_r, coef, base_rows[0], base_rows[1], bias.reshape(steps, 1, LANES))


def tap_rows(med_filter, group_width):
    taps = med_filter.shape[0]
    filters = jnp.transpose(med_filter).astype(jnp.float32)
    groups = LANES // group_width
    zeros = jnp.zeros_like(filters)
    reverse = jnp.concatenate([filters, zeros], axis=1)
    flipped = filters[:, ::-1]
    forward = jnp.concatenate([zeros[:, :1], flipped, zeros[:, 1:]], axis=1)
    return [x.reshape(-1, groups, 2 * taps) for x in (forward, reverse)]


def per_device(size, tokens, feature_table, short_filter, med_filter, med_bias, out_weight):
    taps, groups_local = med_filter.shape
    group_width = feature_table.shape[2] // groups_local
    short_taps = short_filter.shape[1]
    weight = lax.all_gather(out_weight, "seq", axis=0, tiled=True)
    coef = coefficients(feature_table, short_filter)
    coef = lax.all_gather(coef, "ch", axis=2, tiled=True)
    med_all = lax.all_gather(med_filter, "ch", axis=1, tiled=True)
    bias = lax.all_gather(med_bias, "ch", axis=0, tiled=True)
    base_rows = tap_rows(med_all, group_width)
    mixed = hidden(tokens, base_rows, coef, bias, taps, group_width, short_taps, size)
    return jnp.dot(mixed, weight, preferred_element_type=jnp.float32).astype(jnp.bfloat16)


def solution(mesh):
    placed = (
        P("seq"),
        P(None, None, "ch"),
        P(None, None, "ch"),
        P(None, "ch"),
        P("ch"),
        P("seq", "ch"),
    )
    return jax.shard_map(
        functools.partial(per_device, mesh.shape["seq"]),
        mesh=mesh,
        in_specs=placed,
        out_specs=P("seq", "ch"),
        check_vma=False,
    )
```

```python
import functools

import jax
import jax.numpy as jnp
from jax import lax
from jax.experimental import pallas as pl
from jax.experimental.pallas import tpu as pltpu
from jax.sharding import PartitionSpec as P

BASE_CODES = (65, 67, 71, 84)
LANES = 128
MESH = pl.DeviceIdType.MESH


def dot(a, b):
    return jnp.dot(a, b, preferred_element_type=jnp.float32)


def hidden_block(taps, group_width, length, hots, tab, base, columns, group_rows):
    count = hots.shape[1] // (length + taps)
    per_block = length // taps
    groups = LANES // group_width
    lane_group = lax.broadcasted_iota(jnp.int32, (taps, LANES), 1) // group_width
    upper = lax.broadcasted_iota(jnp.int32, (8, LANES), 0) < 4
    short_taps = hots.shape[2] // 8 - 1
    coef = []
    for branch in range(3):
        scale = tab[branch, :, columns]
        feature = tab[3 + branch, :, columns]
        parts = []
        for k in range(short_taps):
            product = scale[k : k + 1] * feature
            high = product.astype(jnp.bfloat16).astype(jnp.float32)
            parts.append(jnp.where(upper, high, product - high))
        parts.append(jnp.zeros((8, LANES), jnp.float32))
        coef.append(jnp.concatenate(parts, axis=0).astype(jnp.bfloat16))
    bias = tab[0, :, columns][7:8]
    pair = jnp.concatenate([coef[0], coef[2]], axis=1)
    window_rows = length + taps
    strands = []
    for strand in range(2):
        first = taps if strand == 0 else 0
        rows = hots[strand]
        both = dot(rows, pair)
        gate = (both[:, :LANES] * both[:, LANES:]).astype(jnp.bfloat16)
        starts = [b * window_rows for b in range(count)]
        middle = dot(
            jnp.concatenate([rows[s + first : s + first + length] for s in starts], axis=0), coef[1]
        )
        window = jnp.concatenate(
            [gate[s + n * taps : s + (n + 2) * taps] for s in starts for n in range(per_block)], axis=1
        )
        mixed = [jnp.zeros((taps, LANES), jnp.float32) for _ in range(count * per_block)]
        taps_here = base[strand, group_rows, :]
        for g in range(groups):
            row = jnp.broadcast_to(taps_here[g : g + 1, :], (taps, 2 * taps))
            toeplitz = pltpu.roll(row, 0, 1, stride=1, stride_axis=0).astype(jnp.bfloat16)
            product = dot(toeplitz, window)
            for n in range(count * per_block):
                mixed[n] = jnp.where(
                    lane_group == g, product[:, n * LANES : (n + 1) * LANES], mixed[n]
                )
        own = jnp.concatenate([gate[s + first : s + first + length] for s in starts], axis=0)
        total = jnp.concatenate(mixed, axis=0) + bias * own.astype(jnp.float32)
        strands.append((middle * total).astype(jnp.bfloat16).astype(jnp.float32))
    return (0.5 * (strands[0] + strands[1])).astype(jnp.bfloat16)


def kernel(
    sizes, taps, group_width,
    hots, tab_in, base_in, weight, out,
    tabs, bases, pieces, mixed, stage,
    tab_send, tab_recv, local_sem, y_send, up_send, down_send, side_send, recv, out_send, out_recv,
):
    seq_size, ch_size = sizes
    outer_size = seq_size // 4
    me, ch = lax.axis_index("seq"), lax.axis_index("ch")
    core = lax.rem(me, 2)
    y = lax.rem(me // 2, 2)
    outer = me // 4
    rows, width = weight.shape
    half = width // 2
    length = out.shape[0]
    tile = min(256, half)
    tiles = half // tile

    def place(o, yy, cc):
        return (o * 2 + yy) * 2 + cc

    side, across = place(outer, y, 1 - core), place(outer, 1 - y, core)

    barrier = pltpu.get_barrier_semaphore()
    for other in (side, across):
        pl.semaphore_signal(barrier, inc=1, device_id={"seq": other}, device_id_type=MESH)
    for step in range(1, ch_size):
        pl.semaphore_signal(
            barrier, inc=1, device_id={"ch": lax.rem(ch + step, ch_size)}, device_id_type=MESH
        )

    @pl.when(outer > 0)
    def _():
        pl.semaphore_signal(barrier, inc=1, device_id={"seq": me - 4}, device_id_type=MESH)

    @pl.when(outer < outer_size - 1)
    def _():
        pl.semaphore_signal(barrier, inc=1, device_id={"seq": me + 4}, device_id_type=MESH)

    ends = (outer > 0).astype(jnp.int32) + (outer < outer_size - 1).astype(jnp.int32)
    pl.semaphore_wait(barrier, ch_size + 1 + ends)

    def remote(src, dst, send, receive, other):
        return pltpu.make_async_remote_copy(
            src_ref=src, dst_ref=dst, send_sem=send, recv_sem=receive,
            device_id=other, device_id_type=MESH,
        )

    def piece(o, yy, cc):
        start = pl.multiple_of((yy * 2 + cc) * rows, rows)
        return pieces.at[o, pl.ds(start, rows)]

    def columns_of(which):
        return weight.at[:, pl.ds(pl.multiple_of(which * half, half), half)]

    def sub_y(sub):
        return y if sub == 0 else 1 - y

    def forwards(origin, sub, action, own=False):
        yy = sub_y(sub)
        dst = piece(origin, yy, core)
        src = columns_of(y) if own else dst
        receive = recv.at[origin, yy * 2 + core]

        @pl.when((origin <= outer) & (outer < outer_size - 1))
        def _():
            action(remote(src, dst, up_send.at[origin, sub], receive, {"seq": me + 4}))

        @pl.when((origin >= outer) & (outer > 0))
        def _():
            action(remote(src, dst, down_send.at[origin, sub], receive, {"seq": me - 4}))

        action(remote(src, dst, side_send.at[origin, sub], receive, {"seq": side}))

    def arrived(origin, slot):
        start = pl.multiple_of(slot * rows, rows)
        dst = pieces.at[origin, pl.ds(start, rows)]
        remote(dst, dst, y_send, recv.at[origin, slot], {"seq": across}).wait_recv()

    y_copy = remote(
        columns_of(1 - y), piece(outer, y, core), y_send, recv.at[outer, y * 2 + core], {"seq": across}
    )
    y_copy.start()
    forwards(outer, 0, lambda c: c.start(), own=True)
    tab_copies = []
    for step in range(1, ch_size):
        other = {"ch": lax.rem(ch + step, ch_size)}
        for number, (src, dst) in enumerate(((tab_in, tabs), (base_in, bases))):
            copy = remote(src, dst.at[ch], tab_send.at[number, step], tab_recv.at[number, ch], other)
            copy.start()
            tab_copies.append(copy)
    local_copies = [
        pltpu.make_async_copy(columns_of(y), piece(outer, y, core), local_sem.at[0]),
        pltpu.make_async_copy(tab_in, tabs.at[ch], local_sem.at[1]),
        pltpu.make_async_copy(base_in, bases.at[ch], local_sem.at[2]),
    ]
    for copy in local_copies:
        copy.start()
    for copy in local_copies:
        copy.wait()

    groups = LANES // group_width
    per_ch = width // LANES
    steps = ch_size * per_ch

    def block(i, carry):
        owner = lax.rem(ch + i // per_ch, ch_size)
        inner = lax.rem(i, per_ch)

        @pl.when((inner == 0) & (i > 0))
        def _():
            for number, dst in enumerate((tabs, bases)):
                remote(
                    dst.at[owner], dst.at[owner], tab_send.at[number, 0],
                    tab_recv.at[number, owner], {"ch": lax.rem(ch + 1, ch_size)},
                ).wait_recv()

        value = hidden_block(
            taps, group_width, length, hots, tabs.at[owner], bases.at[owner],
            pl.ds(pl.multiple_of(inner * LANES, LANES), LANES),
            pl.ds(pl.multiple_of(inner * groups, groups), groups),
        )
        mixed[:, pl.ds(pl.multiple_of((owner * per_ch + inner) * LANES, LANES), LANES)] = value
        return carry

    def event(t, sub):
        yy = sub_y(sub)
        if t == 0:
            arrived(outer, yy * 2 + core)
            forwards(outer, sub, lambda c: c.start())
            return

        @pl.when(outer >= t)
        def _():
            arrived(outer - t, yy * 2 + core)
            forwards(outer - t, sub, lambda c: c.start())

        @pl.when(outer + t < outer_size)
        def _():
            arrived(outer + t, yy * 2 + core)
            forwards(outer + t, sub, lambda c: c.start())

    events = [(t, sub) for t in range(outer_size) for sub in range(2)][1:]
    done = 0
    for number, (t, sub) in enumerate(events):
        upto = steps * (number + 1) // len(events)
        if upto > done:
            lax.fori_loop(done, upto, block, 0)
        done = upto
        event(t, sub)

    def side_wait(o, carry):
        for yy in range(2):
            arrived(o, yy * 2 + 1 - core)
        return carry

    lax.fori_loop(0, outer_size, side_wait, 0)

    depth = 4 * rows

    def product(position, n):
        total = None
        for o in range(outer_size):
            part = dot(
                mixed[position : position + length, o * depth : (o + 1) * depth],
                pieces[o, :, n * tile : (n + 1) * tile],
            )
            total = part if total is None else total + part
        return total.astype(jnp.bfloat16)

    def out_columns(n):
        return out.at[:, pl.ds(pl.multiple_of(y * half + n * tile, tile), tile)]

    out_copies = []
    for n in range(tiles):
        stage[n] = product(length, n)
        copy = remote(stage.at[n], out_columns(n), out_send.at[n], out_recv.at[n], {"seq": across})
        copy.start()
        out_copies.append(copy)
    for n in range(tiles):
        out[:, pl.ds(pl.multiple_of(y * half + n * tile, tile), tile)] = product(0, n)

    y_copy.wait_send()
    for copy in tab_copies:
        copy.wait_send()
    for t in range(outer_size):
        for sub in range(2):
            if t == 0:
                forwards(outer, sub, lambda c: c.wait_send(), own=sub == 0)
                continue

            @pl.when(outer >= t)
            def _():
                forwards(outer - t, sub, lambda c: c.wait_send())

            @pl.when(outer + t < outer_size)
            def _():
                forwards(outer + t, sub, lambda c: c.wait_send())

    for n in range(tiles):
        theirs = out.at[:, pl.ds(pl.multiple_of((1 - y) * half + n * tile, tile), tile)]
        out_copies[n].wait_send()
        remote(stage.at[n], theirs, out_send.at[n], out_recv.at[n], {"seq": across}).wait_recv()


def one_hot(codes, offset, count, step, short_taps):
    picked = jnp.stack(
        [lax.dynamic_slice_in_dim(codes, offset + step * k, count) for k in range(short_taps)], axis=1
    )
    hot = picked[:, :, None] == jnp.arange(8, dtype=jnp.int32) % 4
    hot = jnp.pad(hot, ((0, 0), (0, 1), (0, 0)))
    return hot.reshape(count, 8 * (short_taps + 1)).astype(jnp.bfloat16)


def tap_rows(med_filter):
    filters = jnp.transpose(med_filter).astype(jnp.float32)
    zeros = jnp.zeros_like(filters)
    reverse = jnp.concatenate([filters, zeros], axis=1)
    forward = jnp.concatenate([zeros[:, :1], filters[:, ::-1], zeros[:, 1:]], axis=1)
    return jnp.stack([forward, reverse])


def tables(feature_table, short_filter, med_bias):
    corner = jnp.stack([feature_table[code] for code in BASE_CODES] * 2, axis=1).astype(jnp.float32)
    last = jnp.broadcast_to(med_bias, (3, 1, med_bias.shape[0]))
    return jnp.concatenate([jnp.concatenate([short_filter, last], axis=1), corner], axis=0)


def per_device(sizes, tokens, feature_table, short_filter, med_filter, med_bias, out_weight):
    seq_size, ch_size = sizes
    taps, groups_local = med_filter.shape
    rows, width = out_weight.shape
    group_width = width // groups_local
    short_taps = short_filter.shape[1]
    length = tokens.shape[0]
    window = length + taps
    me = lax.axis_index("seq")
    codes = lax.all_gather(tokens, "seq", axis=0, tiled=True)
    flipped = jnp.pad(3 - codes, (length, length), constant_values=-1)
    codes = jnp.pad(codes, (length, length), constant_values=-1)
    hots = [[], []]
    for index in (me, me ^ 2):
        start = (index + 1) * length
        hots[0].append(one_hot(codes, start - taps, window, -1, short_taps))
        hots[1].append(one_hot(flipped, start, window, 1, short_taps))
    hots = jnp.stack([jnp.concatenate(h, axis=0) for h in hots])
    tab = tables(feature_table, short_filter, med_bias)
    base = tap_rows(med_filter)
    outer_size = seq_size // 4
    half = width // 2
    tile = min(256, half)
    tiles = half // tile
    dma = pltpu.SemaphoreType.DMA
    return pl.pallas_call(
        functools.partial(kernel, sizes, taps, group_width),
        out_shape=jax.ShapeDtypeStruct((length, width), jnp.bfloat16),
        in_specs=[pl.BlockSpec(memory_space=pltpu.VMEM)] * 4,
        out_specs=pl.BlockSpec(memory_space=pltpu.VMEM),
        scratch_shapes=[
            pltpu.VMEM((ch_size,) + tab.shape, jnp.float32),
            pltpu.VMEM((ch_size,) + base.shape, jnp.float32),
            pltpu.VMEM((outer_size, 4 * rows, half), jnp.bfloat16),
            pltpu.VMEM((2 * length, ch_size * width), jnp.bfloat16),
            pltpu.VMEM((tiles, length, tile), jnp.bfloat16),
            dma((2, ch_size)),
            dma((2, ch_size)),
            dma((3,)),
            dma,
            dma((outer_size, 2)),
            dma((outer_size, 2)),
            dma((outer_size, 2)),
            dma((outer_size, 4)),
            dma((tiles,)),
            dma((tiles,)),
        ],
        compiler_params=pltpu.CompilerParams(
            collective_id=0, has_side_effects=True, vmem_limit_bytes=50 * 1024 * 1024
        ),
    )(hots, tab, base, out_weight)


def solution(mesh):
    placed = (
        P("seq"),
        P(None, None, "ch"),
        P(None, None, "ch"),
        P(None, "ch"),
        P("ch"),
        P("seq", "ch"),
    )
    sizes = (mesh.shape["seq"], mesh.shape["ch"])
    return jax.shard_map(
        functools.partial(per_device, sizes),
        mesh=mesh,
        in_specs=placed,
        out_specs=P("seq", "ch"),
        check_vma=False,
    )
```

```python
import functools

import jax
import jax.numpy as jnp
from jax import lax
from jax.experimental import pallas as pl
from jax.experimental.pallas import tpu as pltpu
from jax.sharding import PartitionSpec as P

BASE_CODES = (65, 67, 71, 84)
LANES = 128
MESH = pl.DeviceIdType.MESH


def dot(a, b):
    return jnp.dot(a, b, preferred_element_type=jnp.float32)


def hidden_block(taps, group_width, length, hots, tab, base, columns, group_rows):
    count = hots.shape[1] // (length + taps)
    per_block = length // taps
    groups = LANES // group_width
    lane_group = lax.broadcasted_iota(jnp.int32, (taps, LANES), 1) // group_width
    upper = lax.broadcasted_iota(jnp.int32, (8, LANES), 0) < 4
    short_taps = hots.shape[2] // 8 - 1
    coef = []
    for branch in range(3):
        scale = tab[branch, :, columns]
        feature = tab[3 + branch, :, columns]
        parts = []
        for k in range(short_taps):
            product = scale[k : k + 1] * feature
            high = product.astype(jnp.bfloat16).astype(jnp.float32)
            parts.append(jnp.where(upper, high, product - high))
        parts.append(jnp.zeros((8, LANES), jnp.float32))
        coef.append(jnp.concatenate(parts, axis=0).astype(jnp.bfloat16))
    bias = tab[0, :, columns][7:8]
    pair = jnp.concatenate([coef[0], coef[2]], axis=1)
    window_rows = length + taps
    strands = []
    for strand in range(2):
        first = taps if strand == 0 else 0
        rows = hots[strand]
        both = dot(rows, pair)
        gate = (both[:, :LANES] * both[:, LANES:]).astype(jnp.bfloat16)
        starts = [b * window_rows for b in range(count)]
        middle = dot(
            jnp.concatenate([rows[s + first : s + first + length] for s in starts], axis=0), coef[1]
        )
        window = jnp.concatenate(
            [gate[s + n * taps : s + (n + 2) * taps] for s in starts for n in range(per_block)], axis=1
        )
        mixed = [jnp.zeros((taps, LANES), jnp.float32) for _ in range(count * per_block)]
        taps_here = base[strand, group_rows, :]
        for g in range(groups):
            row = jnp.broadcast_to(taps_here[g : g + 1, :], (taps, 2 * taps))
            toeplitz = pltpu.roll(row, 0, 1, stride=1, stride_axis=0).astype(jnp.bfloat16)
            product = dot(toeplitz, window)
            for n in range(count * per_block):
                mixed[n] = jnp.where(
                    lane_group == g, product[:, n * LANES : (n + 1) * LANES], mixed[n]
                )
        own = jnp.concatenate([gate[s + first : s + first + length] for s in starts], axis=0)
        total = jnp.concatenate(mixed, axis=0) + bias * own.astype(jnp.float32)
        strands.append((middle * total).astype(jnp.bfloat16).astype(jnp.float32))
    return (0.5 * (strands[0] + strands[1])).astype(jnp.bfloat16)


def kernel(
    sizes, taps, group_width,
    hots, tab_in, base_in, weight, out,
    tabs, bases, pieces, mixed, stage,
    tab_send, tab_recv, local_sem, y_send, up_send, down_send, side_send, recv, out_send, out_recv,
):
    seq_size, ch_size = sizes
    outer_size = seq_size // 4
    me, ch = lax.axis_index("seq"), lax.axis_index("ch")
    core = lax.rem(me, 2)
    y = lax.rem(me // 2, 2)
    outer = me // 4
    rows, width = weight.shape
    half = width // 2
    length = out.shape[0]
    tile = min(256, half)
    tiles = half // tile

    def place(o, yy, cc):
        return (o * 2 + yy) * 2 + cc

    side, across = place(outer, y, 1 - core), place(outer, 1 - y, core)

    barrier = pltpu.get_barrier_semaphore()
    for other in (side, across):
        pl.semaphore_signal(barrier, inc=1, device_id={"seq": other}, device_id_type=MESH)
    for step in range(1, ch_size):
        pl.semaphore_signal(
            barrier, inc=1, device_id={"ch": lax.rem(ch + step, ch_size)}, device_id_type=MESH
        )

    @pl.when(outer > 0)
    def _():
        pl.semaphore_signal(barrier, inc=1, device_id={"seq": me - 4}, device_id_type=MESH)

    @pl.when(outer < outer_size - 1)
    def _():
        pl.semaphore_signal(barrier, inc=1, device_id={"seq": me + 4}, device_id_type=MESH)

    ends = (outer > 0).astype(jnp.int32) + (outer < outer_size - 1).astype(jnp.int32)
    pl.semaphore_wait(barrier, ch_size + 1 + ends)

    def remote(src, dst, send, receive, other):
        return pltpu.make_async_remote_copy(
            src_ref=src, dst_ref=dst, send_sem=send, recv_sem=receive,
            device_id=other, device_id_type=MESH,
        )

    def piece(o, yy, cc):
        start = pl.multiple_of((yy * 2 + cc) * rows, rows)
        return pieces.at[o, pl.ds(start, rows)]

    def columns_of(which):
        return weight.at[:, pl.ds(pl.multiple_of(which * half, half), half)]

    def sub_y(sub):
        return y if sub == 0 else 1 - y

    def forwards(origin, sub, action, own=False):
        yy = sub_y(sub)
        dst = piece(origin, yy, core)
        src = columns_of(y) if own else dst
        receive = recv.at[origin, yy * 2 + core]

        @pl.when((origin <= outer) & (outer < outer_size - 1))
        def _():
            action(remote(src, dst, up_send.at[origin, sub], receive, {"seq": me + 4}))

        @pl.when((origin >= outer) & (outer > 0))
        def _():
            action(remote(src, dst, down_send.at[origin, sub], receive, {"seq": me - 4}))

        action(remote(src, dst, side_send.at[origin, sub], receive, {"seq": side}))

    def arrived(origin, slot):
        start = pl.multiple_of(slot * rows, rows)
        dst = pieces.at[origin, pl.ds(start, rows)]
        remote(dst, dst, y_send, recv.at[origin, slot], {"seq": across}).wait_recv()

    y_copy = remote(
        columns_of(1 - y), piece(outer, y, core), y_send, recv.at[outer, y * 2 + core], {"seq": across}
    )
    y_copy.start()
    forwards(outer, 0, lambda c: c.start(), own=True)
    tab_copies = []
    for step in range(1, ch_size):
        other = {"ch": lax.rem(ch + step, ch_size)}
        for number, (src, dst) in enumerate(((tab_in, tabs), (base_in, bases))):
            copy = remote(src, dst.at[ch], tab_send.at[number, step], tab_recv.at[number, ch], other)
            copy.start()
            tab_copies.append(copy)
    local_copies = [
        pltpu.make_async_copy(columns_of(y), piece(outer, y, core), local_sem.at[0]),
        pltpu.make_async_copy(tab_in, tabs.at[ch], local_sem.at[1]),
        pltpu.make_async_copy(base_in, bases.at[ch], local_sem.at[2]),
    ]
    for copy in local_copies:
        copy.start()
    for copy in local_copies:
        copy.wait()

    groups = LANES // group_width
    per_ch = width // LANES
    steps = ch_size * per_ch

    def block(i, carry):
        owner = lax.rem(ch + i // per_ch, ch_size)
        inner = lax.rem(i, per_ch)

        @pl.when((inner == 0) & (i > 0))
        def _():
            for number, dst in enumerate((tabs, bases)):
                remote(
                    dst.at[owner], dst.at[owner], tab_send.at[number, 0],
                    tab_recv.at[number, owner], {"ch": lax.rem(ch + 1, ch_size)},
                ).wait_recv()

        value = hidden_block(
            taps, group_width, length, hots, tabs.at[owner], bases.at[owner],
            pl.ds(pl.multiple_of(inner * LANES, LANES), LANES),
            pl.ds(pl.multiple_of(inner * groups, groups), groups),
        )
        mixed[:, pl.ds(pl.multiple_of((owner * per_ch + inner) * LANES, LANES), LANES)] = value
        return carry

    def event(t, sub):
        yy = sub_y(sub)
        if t == 0:
            arrived(outer, yy * 2 + core)
            forwards(outer, sub, lambda c: c.start())
            return

        @pl.when(outer >= t)
        def _():
            arrived(outer - t, yy * 2 + core)
            forwards(outer - t, sub, lambda c: c.start())

        @pl.when(outer + t < outer_size)
        def _():
            arrived(outer + t, yy * 2 + core)
            forwards(outer + t, sub, lambda c: c.start())

    events = [(t, sub) for t in range(outer_size) for sub in range(2)][1:]
    done = 0
    for number, (t, sub) in enumerate(events):
        upto = steps * (number + 1) // len(events)
        if upto > done:
            lax.fori_loop(done, upto, block, 0)
        done = upto
        event(t, sub)

    def side_wait(o, carry):
        for yy in range(2):
            arrived(o, yy * 2 + 1 - core)
        return carry

    lax.fori_loop(0, outer_size, side_wait, 0)

    depth = 4 * rows

    def product(position, n):
        total = None
        for o in range(outer_size):
            part = dot(
                mixed[position : position + length, o * depth : (o + 1) * depth],
                pieces[o, :, n * tile : (n + 1) * tile],
            )
            total = part if total is None else total + part
        return total.astype(jnp.bfloat16)

    def out_columns(n):
        return out.at[:, pl.ds(pl.multiple_of(y * half + n * tile, tile), tile)]

    out_copies = []
    for n in range(tiles):
        stage[n] = product(length, n)
        copy = remote(stage.at[n], out_columns(n), out_send.at[n], out_recv.at[n], {"seq": across})
        copy.start()
        out_copies.append(copy)
    for n in range(tiles):
        out[:, pl.ds(pl.multiple_of(y * half + n * tile, tile), tile)] = product(0, n)

    y_copy.wait_send()
    for copy in tab_copies:
        copy.wait_send()
    for t in range(outer_size):
        for sub in range(2):
            if t == 0:
                forwards(outer, sub, lambda c: c.wait_send(), own=sub == 0)
                continue

            @pl.when(outer >= t)
            def _():
                forwards(outer - t, sub, lambda c: c.wait_send())

            @pl.when(outer + t < outer_size)
            def _():
                forwards(outer + t, sub, lambda c: c.wait_send())

    for n in range(tiles):
        theirs = out.at[:, pl.ds(pl.multiple_of((1 - y) * half + n * tile, tile), tile)]
        out_copies[n].wait_send()
        remote(stage.at[n], theirs, out_send.at[n], out_recv.at[n], {"seq": across}).wait_recv()


def one_hot(codes, offset, count, step, short_taps):
    picked = jnp.stack(
        [codes[offset + step * k : offset + step * k + count] for k in range(short_taps)], axis=1
    )
    hot = picked[:, :, None] == jnp.arange(8, dtype=jnp.int32) % 4
    hot = jnp.pad(hot, ((0, 0), (0, 1), (0, 0)))
    return hot.reshape(count, 8 * (short_taps + 1)).astype(jnp.bfloat16)


def tap_rows(med_filter):
    filters = jnp.transpose(med_filter).astype(jnp.float32)
    zeros = jnp.zeros_like(filters)
    reverse = jnp.concatenate([filters, zeros], axis=1)
    forward = jnp.concatenate([zeros[:, :1], filters[:, ::-1], zeros[:, 1:]], axis=1)
    return jnp.stack([forward, reverse])


def tables(feature_table, short_filter, med_bias):
    corner = jnp.stack([feature_table[code] for code in BASE_CODES] * 2, axis=1).astype(jnp.float32)
    last = jnp.broadcast_to(med_bias, (3, 1, med_bias.shape[0]))
    return jnp.concatenate([jnp.concatenate([short_filter, last], axis=1), corner], axis=0)


def per_device(sizes, tokens, feature_table, short_filter, med_filter, med_bias, out_weight):
    seq_size, ch_size = sizes
    taps, groups_local = med_filter.shape
    rows, width = out_weight.shape
    group_width = width // groups_local
    short_taps = short_filter.shape[1]
    length = tokens.shape[0]
    window = length + taps
    me = lax.axis_index("seq")
    before = lax.ppermute(tokens, "seq", [(i, i + 1) for i in range(seq_size - 1)])
    after = lax.ppermute(tokens, "seq", [(i + 1, i) for i in range(seq_size - 1)])
    before = jnp.where(me == 0, -1, before)
    after = jnp.where(me == seq_size - 1, -1, after)
    mine = jnp.concatenate([before, tokens, after])
    theirs = lax.ppermute(mine, "seq", [(i, i ^ 2) for i in range(seq_size)])
    hots = [[], []]
    for codes in (mine, theirs):
        flipped = jnp.where(codes < 0, -1, 3 - codes)
        hots[0].append(one_hot(codes, length - taps, window, -1, short_taps))
        hots[1].append(one_hot(flipped, length, window, 1, short_taps))
    hots = jnp.stack([jnp.concatenate(h, axis=0) for h in hots])
    tab = tables(feature_table, short_filter, med_bias)
    base = tap_rows(med_filter)
    outer_size = seq_size // 4
    half = width // 2
    tile = min(256, half)
    tiles = half // tile
    dma = pltpu.SemaphoreType.DMA
    return pl.pallas_call(
        functools.partial(kernel, sizes, taps, group_width),
        out_shape=jax.ShapeDtypeStruct((length, width), jnp.bfloat16),
        in_specs=[pl.BlockSpec(memory_space=pltpu.VMEM)] * 4,
        out_specs=pl.BlockSpec(memory_space=pltpu.VMEM),
        scratch_shapes=[
            pltpu.VMEM((ch_size,) + tab.shape, jnp.float32),
            pltpu.VMEM((ch_size,) + base.shape, jnp.float32),
            pltpu.VMEM((outer_size, 4 * rows, half), jnp.bfloat16),
            pltpu.VMEM((2 * length, ch_size * width), jnp.bfloat16),
            pltpu.VMEM((tiles, length, tile), jnp.bfloat16),
            dma((2, ch_size)),
            dma((2, ch_size)),
            dma((3,)),
            dma,
            dma((outer_size, 2)),
            dma((outer_size, 2)),
            dma((outer_size, 2)),
            dma((outer_size, 4)),
            dma((tiles,)),
            dma((tiles,)),
        ],
        compiler_params=pltpu.CompilerParams(
            collective_id=0, has_side_effects=True, vmem_limit_bytes=50 * 1024 * 1024
        ),
    )(hots, tab, base, out_weight)


def solution(mesh):
    placed = (
        P("seq"),
        P(None, None, "ch"),
        P(None, None, "ch"),
        P(None, "ch"),
        P("ch"),
        P("seq", "ch"),
    )
    sizes = (mesh.shape["seq"], mesh.shape["ch"])
    return jax.shard_map(
        functools.partial(per_device, sizes),
        mesh=mesh,
        in_specs=placed,
        out_specs=P("seq", "ch"),
        check_vma=False,
    )
```

```python
import functools

import jax
import jax.numpy as jnp
from jax import lax
from jax.experimental import pallas as pl
from jax.experimental.pallas import tpu as pltpu
from jax.sharding import PartitionSpec as P

BASE_CODES = (65, 67, 71, 84)
LANES = 128
MESH = pl.DeviceIdType.MESH


def dot(a, b):
    return jnp.dot(a, b, preferred_element_type=jnp.float32)


def hidden_block(taps, group_width, length, hots, tab, base, columns, group_rows):
    count = hots.shape[1] // (length + taps)
    per_block = length // taps
    groups = LANES // group_width
    lane_group = lax.broadcasted_iota(jnp.int32, (taps, LANES), 1) // group_width
    upper = lax.broadcasted_iota(jnp.int32, (8, LANES), 0) < 4
    short_taps = hots.shape[2] // 8 - 1
    coef = []
    for branch in range(3):
        scale = tab[branch, :, columns]
        feature = tab[3 + branch, :, columns]
        parts = []
        for k in range(short_taps):
            product = scale[k : k + 1] * feature
            high = product.astype(jnp.bfloat16).astype(jnp.float32)
            parts.append(jnp.where(upper, high, product - high))
        parts.append(jnp.zeros((8, LANES), jnp.float32))
        coef.append(jnp.concatenate(parts, axis=0).astype(jnp.bfloat16))
    bias = tab[0, :, columns][7:8]
    pair = jnp.concatenate([coef[0], coef[2]], axis=1)
    window_rows = length + taps
    strands = []
    for strand in range(2):
        first = taps if strand == 0 else 0
        rows = hots[strand]
        both = dot(rows, pair)
        gate = (both[:, :LANES] * both[:, LANES:]).astype(jnp.bfloat16)
        starts = [b * window_rows for b in range(count)]
        middle = dot(
            jnp.concatenate([rows[s + first : s + first + length] for s in starts], axis=0), coef[1]
        )
        window = jnp.concatenate(
            [gate[s + n * taps : s + (n + 2) * taps] for s in starts for n in range(per_block)], axis=1
        )
        mixed = [jnp.zeros((taps, LANES), jnp.float32) for _ in range(count * per_block)]
        taps_here = base[strand, group_rows, :]
        for g in range(groups):
            row = jnp.broadcast_to(taps_here[g : g + 1, :], (taps, 2 * taps))
            toeplitz = pltpu.roll(row, 0, 1, stride=1, stride_axis=0).astype(jnp.bfloat16)
            product = dot(toeplitz, window)
            for n in range(count * per_block):
                mixed[n] = jnp.where(
                    lane_group == g, product[:, n * LANES : (n + 1) * LANES], mixed[n]
                )
        own = jnp.concatenate([gate[s + first : s + first + length] for s in starts], axis=0)
        total = jnp.concatenate(mixed, axis=0) + bias * own.astype(jnp.float32)
        strands.append((middle * total).astype(jnp.bfloat16).astype(jnp.float32))
    return (0.5 * (strands[0] + strands[1])).astype(jnp.bfloat16)


def kernel(
    sizes, taps, group_width,
    hots, tab_in, base_in, weight, out,
    tabs, bases, pieces, mixed, stage,
    tab_send, tab_recv, local_sem, y_send, up_send, down_send, side_send, recv, out_send, out_recv,
):
    seq_size, ch_size = sizes
    outer_size = seq_size // 4
    me, ch = lax.axis_index("seq"), lax.axis_index("ch")
    core = lax.rem(me, 2)
    y = lax.rem(me // 2, 2)
    outer = me // 4
    rows, width = weight.shape
    half = width // 2
    length = out.shape[0]
    parts, _, _, part_width = pieces.shape
    tile = min(256, part_width)
    part_tiles = part_width // tile
    tiles = half // tile

    def place(o, yy, cc):
        return (o * 2 + yy) * 2 + cc

    side, across = place(outer, y, 1 - core), place(outer, 1 - y, core)

    barrier = pltpu.get_barrier_semaphore()
    for other in (side, across):
        pl.semaphore_signal(barrier, inc=1, device_id={"seq": other}, device_id_type=MESH)
    for step in range(1, ch_size):
        pl.semaphore_signal(
            barrier, inc=1, device_id={"ch": lax.rem(ch + step, ch_size)}, device_id_type=MESH
        )

    @pl.when(outer > 0)
    def _():
        pl.semaphore_signal(barrier, inc=1, device_id={"seq": me - 4}, device_id_type=MESH)

    @pl.when(outer < outer_size - 1)
    def _():
        pl.semaphore_signal(barrier, inc=1, device_id={"seq": me + 4}, device_id_type=MESH)

    ends = (outer > 0).astype(jnp.int32) + (outer < outer_size - 1).astype(jnp.int32)
    pl.semaphore_wait(barrier, ch_size + 1 + ends)

    def remote(src, dst, send, receive, other):
        return pltpu.make_async_remote_copy(
            src_ref=src, dst_ref=dst, send_sem=send, recv_sem=receive,
            device_id=other, device_id_type=MESH,
        )

    def piece(part, o, yy, cc):
        start = pl.multiple_of((yy * 2 + cc) * rows, rows)
        return pieces.at[part, o, pl.ds(start, rows)]

    def columns_of(part, which):
        start = pl.multiple_of(which * half + part * part_width, part_width)
        return weight.at[:, pl.ds(start, part_width)]

    def sub_y(sub):
        return y if sub == 0 else 1 - y

    def forwards(part, origin, sub, action, own=False):
        yy = sub_y(sub)
        dst = piece(part, origin, yy, core)
        src = columns_of(part, y) if own else dst
        receive = recv.at[part, origin, yy * 2 + core]

        @pl.when((origin <= outer) & (outer < outer_size - 1))
        def _():
            action(remote(src, dst, up_send.at[part, origin, sub], receive, {"seq": me + 4}))

        @pl.when((origin >= outer) & (outer > 0))
        def _():
            action(remote(src, dst, down_send.at[part, origin, sub], receive, {"seq": me - 4}))

        action(remote(src, dst, side_send.at[part, origin, sub], receive, {"seq": side}))

    def arrived(part, origin, slot):
        start = pl.multiple_of(slot * rows, rows)
        dst = pieces.at[part, origin, pl.ds(start, rows)]
        remote(dst, dst, y_send.at[part], recv.at[part, origin, slot], {"seq": across}).wait_recv()

    def start(copy):
        copy.start()

    def wait_send(copy):
        copy.wait_send()

    y_copies = [
        remote(
            columns_of(part, 1 - y), piece(part, outer, y, core), y_send.at[part],
            recv.at[part, outer, y * 2 + core], {"seq": across},
        )
        for part in range(parts)
    ]
    y_copies[0].start()
    forwards(0, outer, 0, start, own=True)
    for copy in y_copies[1:]:
        copy.start()
    tab_copies = []
    for step in range(1, ch_size):
        other = {"ch": lax.rem(ch + step, ch_size)}
        for number, (src, dst) in enumerate(((tab_in, tabs), (base_in, bases))):
            copy = remote(src, dst.at[ch], tab_send.at[number, step], tab_recv.at[number, ch], other)
            copy.start()
            tab_copies.append(copy)
    local_copies = [
        pltpu.make_async_copy(tab_in, tabs.at[ch], local_sem.at[0]),
        pltpu.make_async_copy(base_in, bases.at[ch], local_sem.at[1]),
    ] + [
        pltpu.make_async_copy(
            columns_of(part, y), piece(part, outer, y, core), local_sem.at[2 + part]
        )
        for part in range(parts)
    ]
    for copy in local_copies:
        copy.start()
    for copy in local_copies:
        copy.wait()

    groups = LANES // group_width
    per_ch = width // LANES
    steps = ch_size * per_ch

    def block(i, carry):
        owner = lax.rem(ch + i // per_ch, ch_size)
        inner = lax.rem(i, per_ch)

        @pl.when((inner == 0) & (i > 0))
        def _():
            for number, dst in enumerate((tabs, bases)):
                remote(
                    dst.at[owner], dst.at[owner], tab_send.at[number, 0],
                    tab_recv.at[number, owner], {"ch": lax.rem(ch + 1, ch_size)},
                ).wait_recv()

        value = hidden_block(
            taps, group_width, length, hots, tabs.at[owner], bases.at[owner],
            pl.ds(pl.multiple_of(inner * LANES, LANES), LANES),
            pl.ds(pl.multiple_of(inner * groups, groups), groups),
        )
        mixed[:, pl.ds(pl.multiple_of((owner * per_ch + inner) * LANES, LANES), LANES)] = value
        return carry

    def event(part, t, sub):
        yy = sub_y(sub)
        if t == 0:
            if sub == 1:
                arrived(part, outer, yy * 2 + core)
            forwards(part, outer, sub, start, own=sub == 0)
            return

        @pl.when(outer >= t)
        def _():
            arrived(part, outer - t, yy * 2 + core)
            forwards(part, outer - t, sub, start)

        @pl.when(outer + t < outer_size)
        def _():
            arrived(part, outer + t, yy * 2 + core)
            forwards(part, outer + t, sub, start)

    both = (0, 1)
    events = [(0, t, sub) for t in range(outer_size - 1) for sub in both][1:]
    for part in range(1, parts):
        events += [(part, 0, sub) for sub in both]
        events += [(part - 1, outer_size - 1, sub) for sub in both]
        events += [(part, t, sub) for t in range(1, outer_size - 1) for sub in both]
    last = [(parts - 1, outer_size - 1, sub) for sub in both]
    due = {}
    for number, item in enumerate(events):
        due.setdefault(max(0, steps * (number + 1) // len(events) - 1), []).append(item)

    def step(i, carry):
        block(i, carry)
        for when, items in due.items():

            @pl.when(i == when)
            def _():
                for item in items:
                    event(*item)

        return carry

    lax.fori_loop(0, steps, step, 0)
    depth = 4 * rows

    def side_waits(part):
        def wait(o, carry):
            for yy in both:
                arrived(part, o, yy * 2 + 1 - core)
            return carry

        lax.fori_loop(0, outer_size, wait, 0)

    def product(position, n):
        part, inside = n // part_tiles, n % part_tiles
        total = None
        for o in range(outer_size):
            term = dot(
                mixed[position : position + length, o * depth : (o + 1) * depth],
                pieces[part, o, :, inside * tile : (inside + 1) * tile],
            )
            total = term if total is None else total + term
        return total.astype(jnp.bfloat16)

    def out_columns(which, n):
        return pl.ds(pl.multiple_of(which * half + n * tile, tile), tile)

    out_copies = []
    for part in range(parts):
        numbers = range(part * part_tiles, (part + 1) * part_tiles)
        final = part == parts - 1
        if final:
            for item in last[1:]:
                event(*item)
        side_waits(part)
        for n in numbers:
            stage[n] = product(length, n)
            copy = remote(
                stage.at[n], out.at[:, out_columns(y, n)], out_send.at[n], out_recv.at[n], {"seq": across}
            )
            copy.start()
            out_copies.append(copy)
        if part == parts - 2:
            event(*last[0])
        for n in numbers:
            out[:, out_columns(y, n)] = product(0, n)

    for copy in y_copies + tab_copies:
        copy.wait_send()
    for part in range(parts):
        for t in range(outer_size):
            for sub in both:
                if t == 0:
                    forwards(part, outer, sub, wait_send, own=sub == 0)
                    continue

                @pl.when(outer >= t)
                def _():
                    forwards(part, outer - t, sub, wait_send)

                @pl.when(outer + t < outer_size)
                def _():
                    forwards(part, outer + t, sub, wait_send)

    for n in range(tiles):
        out_copies[n].wait_send()
        remote(
            stage.at[n], out.at[:, out_columns(1 - y, n)], out_send.at[n], out_recv.at[n], {"seq": across}
        ).wait_recv()


def one_hot(codes, offset, count, step, short_taps):
    picked = jnp.stack(
        [codes[offset + step * k : offset + step * k + count] for k in range(short_taps)], axis=1
    )
    hot = picked[:, :, None] == jnp.arange(8, dtype=jnp.int32) % 4
    hot = jnp.pad(hot, ((0, 0), (0, 1), (0, 0)))
    return hot.reshape(count, 8 * (short_taps + 1)).astype(jnp.bfloat16)


def tap_rows(med_filter):
    filters = jnp.transpose(med_filter).astype(jnp.float32)
    zeros = jnp.zeros_like(filters)
    reverse = jnp.concatenate([filters, zeros], axis=1)
    forward = jnp.concatenate([zeros[:, :1], filters[:, ::-1], zeros[:, 1:]], axis=1)
    return jnp.stack([forward, reverse])


def tables(feature_table, short_filter, med_bias):
    corner = jnp.stack([feature_table[code] for code in BASE_CODES] * 2, axis=1).astype(jnp.float32)
    last = jnp.broadcast_to(med_bias, (3, 1, med_bias.shape[0]))
    return jnp.concatenate([jnp.concatenate([short_filter, last], axis=1), corner], axis=0)


def per_device(sizes, tokens, feature_table, short_filter, med_filter, med_bias, out_weight):
    seq_size, ch_size = sizes
    taps, groups_local = med_filter.shape
    rows, width = out_weight.shape
    group_width = width // groups_local
    short_taps = short_filter.shape[1]
    length = tokens.shape[0]
    window = length + taps
    me = lax.axis_index("seq")
    before = lax.ppermute(tokens, "seq", [(i, i + 1) for i in range(seq_size - 1)])
    after = lax.ppermute(tokens, "seq", [(i + 1, i) for i in range(seq_size - 1)])
    before = jnp.where(me == 0, -1, before)
    after = jnp.where(me == seq_size - 1, -1, after)
    mine = jnp.concatenate([before, tokens, after])
    theirs = lax.ppermute(mine, "seq", [(i, i ^ 2) for i in range(seq_size)])
    hots = [[], []]
    for codes in (mine, theirs):
        flipped = jnp.where(codes < 0, -1, 3 - codes)
        hots[0].append(one_hot(codes, length - taps, window, -1, short_taps))
        hots[1].append(one_hot(flipped, length, window, 1, short_taps))
    hots = jnp.stack([jnp.concatenate(h, axis=0) for h in hots])
    tab = tables(feature_table, short_filter, med_bias)
    base = tap_rows(med_filter)
    outer_size = seq_size // 4
    half = width // 2
    parts = 2
    tile = min(256, half // parts)
    tiles = half // tile
    dma = pltpu.SemaphoreType.DMA
    return pl.pallas_call(
        functools.partial(kernel, sizes, taps, group_width),
        out_shape=jax.ShapeDtypeStruct((length, width), jnp.bfloat16),
        in_specs=[pl.BlockSpec(memory_space=pltpu.VMEM)] * 4,
        out_specs=pl.BlockSpec(memory_space=pltpu.VMEM),
        scratch_shapes=[
            pltpu.VMEM((ch_size,) + tab.shape, jnp.float32),
            pltpu.VMEM((ch_size,) + base.shape, jnp.float32),
            pltpu.VMEM((parts, outer_size, 4 * rows, half // parts), jnp.bfloat16),
            pltpu.VMEM((2 * length, ch_size * width), jnp.bfloat16),
            pltpu.VMEM((tiles, length, tile), jnp.bfloat16),
            dma((2, ch_size)),
            dma((2, ch_size)),
            dma((2 + parts,)),
            dma((parts,)),
            dma((parts, outer_size, 2)),
            dma((parts, outer_size, 2)),
            dma((parts, outer_size, 2)),
            dma((parts, outer_size, 4)),
            dma((tiles,)),
            dma((tiles,)),
        ],
        compiler_params=pltpu.CompilerParams(
            collective_id=0, has_side_effects=True, vmem_limit_bytes=50 * 1024 * 1024
        ),
    )(hots, tab, base, out_weight)


def solution(mesh):
    placed = (
        P("seq"),
        P(None, None, "ch"),
        P(None, None, "ch"),
        P(None, "ch"),
        P("ch"),
        P("seq", "ch"),
    )
    sizes = (mesh.shape["seq"], mesh.shape["ch"])
    return jax.shard_map(
        functools.partial(per_device, sizes),
        mesh=mesh,
        in_specs=placed,
        out_specs=P("seq", "ch"),
        check_vma=False,
    )
```
